32 devices in a mesh: chain: 4 (over z), tech: 4 (over x, core), blk: 2 (over y).
Axes of the slice: x: 2, y: 2, z: 4, core: 2. Of those that a mesh axis runs over, the one named last changes fastest.
Arguments:
- block_inverse: bfloat16 [4, 4, 3072, 3072], P('tech', 'chain', 'blk'), may hold values from -1 to 4.5, as said below
- coupling: bfloat16 [4, 4, 3072, 512], P('tech', 'chain', 'blk'), may hold values from -0.0390625 to 0.0390625
- data_rhs: bfloat16 [4, 4, 3072, 256], P('tech', 'chain', 'blk'), may hold values from -6 to 6
- station_seen: int32 [4, 4, 1024], P('tech', 'chain', 'blk'), may hold values 0 or 1
- shared_inverse: float32 [4, 512, 512], P('chain'), may hold values from -0.05 to 1, as said below
- walk_weight: float32 [512], replicated, may hold values from 0.92 to 1
- shared_rhs: float32 [4, 512, 256], P('chain'), may hold values from -1.2 to 1.2
Outputs:
- coords: float32 [4, 4, 3072, 256], P('tech', 'chain', 'blk')
- shared: float32 [4, 512, 256], P('chain')
The draws below stay inside these ranges and needn't reach their ends.
Inputs may be any that keep to these rules, and one draw needn't show every extreme that they name: `block_inverse`: each block is symmetric. `shared_inverse`: each block is symmetric.
All inputs are finite; a program needn't handle non-finite values. No bound on the sum of `station_seen` on one device may be relied on, other than what follows from the above.
Results may differ from the reference program's by a relative error of at most 0.004.
Values may be sent and summed in bfloat16 or wider, within the bound.
A program may use at most 128 MiB of HBM per device.

```python
import math
import jax
import jax.numpy as jnp
from jax import lax

STATIONS = 1024
SHARED = 512
SAMPLES = 256
SWEEPS = 2
B = 3072
WEEKS = 4
GROUPS = 4


def symmetric_block(block_key, order, diag_low, diag_high, spread):
    first_key, second_key = jax.random.split(block_key)
    diagonal = jnp.exp(jax.random.uniform(first_key, (order,), jnp.float32, jnp.log(diag_low), jnp.log(diag_high)))
    noise = jax.random.normal(second_key, (order, order), jnp.float32)
    noise = jnp.clip((noise + noise.T) * 0.7071067811865476, -4.0, 4.0) * (spread / jnp.sqrt(1.0 * order))
    root = jnp.sqrt(diagonal)
    return jnp.diag(diagonal) + root[:, None] * noise * root[None, :]


def draw_block_inverse(key, part):
    bounds = (0.5, 2.0)

    def one_block(index):
        block = symmetric_block(jax.random.fold_in(jax.random.fold_in(key, 11), index), B, bounds[0], bounds[1], 0.35)
        return block.astype(jnp.bfloat16)
    flat = lax.map(one_block, jnp.arange(GROUPS * WEEKS, dtype=jnp.int32))
    return flat.reshape(GROUPS, WEEKS, B, B)


def draw_shared_inverse(key, part):
    bounds = (0.82, 0.92)
    spread = 0.05

    def one_week(index):
        week_key = jax.random.fold_in(jax.random.fold_in(key, 23), index)
        first_key, second_key = jax.random.split(week_key)
        diagonal = jax.random.uniform(first_key, (SHARED,), jnp.float32, bounds[0], bounds[1])
        noise = jax.random.normal(second_key, (SHARED, SHARED), jnp.float32)
        noise = jnp.clip((noise + noise.T) * 0.7071067811865476, -4.0, 4.0) * (spread / jnp.sqrt(1.0 * SHARED))
        return jnp.diag(diagonal) + noise
    return lax.map(one_week, jnp.arange(WEEKS, dtype=jnp.int32))


def with_ends(array, rng, least, top_value):
    index_at = [jax.random.randint(jax.random.fold_in(rng, axis), (), 0, length) for axis, length in enumerate(array.shape)]
    main_axis = array.shape.index(max(array.shape))
    next_to = index_at[:main_axis] + [(index_at[main_axis] + 1) % array.shape[main_axis]] + index_at[main_axis + 1:]
    return array.at[tuple(index_at)].set(least).at[tuple(next_to)].set(top_value)


def block_levels(key, dims, cuts, low, high):
    gain, own = 1.0, jax.random.fold_in(key, 6)
    for dim, shards_of in cuts:
        steps = jnp.exp(jax.random.uniform(jax.random.fold_in(own, dim), (shards_of,), jnp.float32, low / len(cuts), high / len(cuts)))
        gain = gain * jnp.repeat(steps, dims[dim] // shards_of).reshape([-1 if axis == dim else 1 for axis in range(len(dims))])
    return gain


def centred(own_key, extent, width, reach, cuts=(), kind=jnp.bfloat16):
    loudness = block_levels(own_key, extent, cuts, -0.22, 0.18) if cuts else 1.0
    entries = jax.random.normal(own_key, extent, jnp.float32) * width * loudness
    return jnp.minimum(jnp.maximum(entries, -reach), reach).astype(kind)


def setup_inputs(seed: int = 0) -> dict:
    arg_keys = jax.random.split(jax.random.key(seed), 8)
    block_inverse = draw_block_inverse(jax.random.fold_in(arg_keys[7], 71), 0)
    coupling = centred(arg_keys[1], (GROUPS, WEEKS, B, SHARED), (8 * B) ** -0.5, 0.0390625, ((0, 4), (1, 4), (2, 2)))
    data_rhs = centred(arg_keys[2], (GROUPS, WEEKS, B, SAMPLES), 1.0, 6.0, ((0, 4), (1, 4), (2, 2)))
    station_seen = with_ends((jax.random.randint(arg_keys[3], (GROUPS, WEEKS, STATIONS), 0, 4) < 3).astype(jnp.int32), jax.random.fold_in(arg_keys[3], 1), 0, 1)
    shared_inverse = draw_shared_inverse(jax.random.fold_in(arg_keys[7], 71), 0)
    walk_weight = jnp.clip(jnp.exp(jax.random.uniform(arg_keys[5], (SHARED,), jnp.float32, math.log(0.92), math.log(1.0))), 0.92, 1.0)
    shared_rhs = centred(arg_keys[6], (WEEKS, SHARED, SAMPLES), 0.2, 1.2, ((0, 4),), jnp.float32)
    return {"block_inverse": block_inverse, "coupling": coupling, "data_rhs": data_rhs, "station_seen": station_seen, "shared_inverse": shared_inverse, "walk_weight": walk_weight, "shared_rhs": shared_rhs}


def reference(block_inverse, coupling, data_rhs, station_seen, shared_inverse, walk_weight, shared_rhs):
    blocks = GROUPS * WEEKS
    flat_inverse = block_inverse.reshape(blocks, B, B)
    flat_coupling = coupling.reshape(blocks, B, SHARED)
    flat_rhs = data_rhs.reshape(blocks, B, SAMPLES)
    flat_seen = jnp.repeat(station_seen, 3, axis=-1).astype(jnp.float32).reshape(blocks, B)
    step_matrix = shared_inverse * walk_weight[None, None, :]
    shared = jnp.zeros((WEEKS, SHARED, SAMPLES), jnp.float32)
    coords = jnp.zeros((blocks, B, SAMPLES), jnp.float32)
    for sweep_index in range(SWEEPS):
        later = jnp.concatenate([shared[1:], jnp.zeros((1, SHARED, SAMPLES), jnp.float32)], axis=0)
        shared_low = shared.astype(jnp.bfloat16)

        def solve_block(index):
            week = index % WEEKS
            product = jnp.dot(flat_coupling[index], shared_low[week], preferred_element_type=jnp.float32)
            residual_low = (flat_rhs[index].astype(jnp.float32) - product).astype(jnp.bfloat16)
            solved = flat_seen[index][:, None] * jnp.dot(flat_inverse[index], residual_low, preferred_element_type=jnp.float32)
            term = jnp.dot(flat_coupling[index].T, solved.astype(jnp.bfloat16), preferred_element_type=jnp.float32)
            return solved, term

        coords, terms = lax.map(solve_block, jnp.arange(blocks, dtype=jnp.int32))
        station_sum = terms.reshape(GROUPS, WEEKS, SHARED, SAMPLES).sum(axis=0)
        offsets = jnp.matmul(shared_inverse, shared_rhs + walk_weight[None, :, None] * later - station_sum, precision=lax.Precision.HIGHEST)

        def advance(previous, pieces):
            offset, matrix = pieces
            current = offset + jnp.dot(matrix, previous, precision=lax.Precision.HIGHEST)
            return current, current

        _, shared = lax.scan(advance, jnp.zeros((SHARED, SAMPLES), jnp.float32), (offsets, step_matrix))
    return coords.reshape(GROUPS, WEEKS, B, SAMPLES), shared
```

```python
import functools

import jax
import jax.numpy as jnp
from jax import lax
from jax.experimental import pallas as pl
from jax.experimental.pallas import tpu as pltpu
from jax.sharding import PartitionSpec as P

SWEEPS = 2
F32 = jnp.float32
BF16 = jnp.bfloat16
NT = (((1,), (1,)), ((), ()))
TN = (((0,), (0,)), ((), ()))


def split_two(value):
    high = value.astype(BF16)
    return high, (value - high.astype(F32)).astype(BF16)


def kernel(
    weeks,
    groups,
    parts,
    chunk,
    tile,
    inverse_hbm,
    coupling_hbm,
    rhs_hbm,
    seen_ref,
    week_inverse_ref,
    walk_ref,
    week_rhs_ref,
    coords_hbm,
    shared_ref,
    inverse,
    coupling,
    rhs,
    residual,
    arrived,
    coords,
    coords_low,
    seen,
    week_rhs,
    inverse_high,
    inverse_low,
    terms,
    terms_low,
    terms_in,
    shared_low,
    current,
    previous,
    later,
    local_sem,
    gather_send,
    gather_recv,
    terms_send,
    terms_recv,
    shared_send,
    shared_recv,
    chain_send,
    chain_recv,
):
    week = lax.axis_index("chain")
    group = lax.axis_index("tech")
    part = lax.axis_index("blk")
    team = groups * parts
    rank = group * parts + part
    rows = rhs.shape[0]
    piece = current.shape[1]
    chunks = rows // chunk
    not_first = week > 0
    not_last = week < weeks - 1

    def member(number):
        return {"tech": number // parts, "blk": lax.rem(number, parts)}

    def ahead(distance):
        return lax.rem(rank + distance, team)

    def behind(distance):
        return lax.rem(rank + team - distance, team)

    def own_slice(number):
        return pl.ds(pl.multiple_of(number * piece, piece), piece)

    loads = []
    loads.append(pltpu.make_async_copy(rhs_hbm, rhs, local_sem.at[0]))
    for slot in range(parts):
        column = pl.multiple_of(lax.rem(part + parts - slot, parts) * rows, 128)
        loads.append(
            pltpu.make_async_copy(
                inverse_hbm.at[:, pl.ds(column, rows)], inverse.at[slot], local_sem.at[1 + slot]
            )
        )
    loads.append(pltpu.make_async_copy(coupling_hbm, coupling, local_sem.at[1 + parts]))
    for load in loads:
        load.start()

    barrier = pltpu.get_barrier_semaphore()
    for distance in range(1, team):
        pl.semaphore_signal(barrier, inc=1, device_id=member(ahead(distance)))

    @pl.when(not_first)
    def _():
        pl.semaphore_signal(barrier, inc=1, device_id={"chain": week - 1})

    @pl.when(not_last)
    def _():
        pl.semaphore_signal(barrier, inc=1, device_id={"chain": week + 1})

    pl.semaphore_wait(
        barrier, team - 1 + not_first.astype(jnp.int32) + not_last.astype(jnp.int32)
    )

    def gather_copy(sweep, distance, index):
        source = rhs_hbm if sweep == 0 else residual
        span = pl.ds(index * chunk, chunk)
        return pltpu.make_async_remote_copy(
            src_ref=source.at[span],
            dst_ref=arrived.at[sweep, distance - 1, span],
            send_sem=gather_send.at[sweep, distance - 1, index],
            recv_sem=gather_recv.at[sweep, distance - 1, index],
            device_id={"blk": lax.rem(part + distance, parts)},
        )

    def terms_copy(sweep, distance):
        return pltpu.make_async_remote_copy(
            src_ref=terms_low.at[sweep, own_slice(ahead(distance))],
            dst_ref=terms_in.at[sweep, distance - 1],
            send_sem=terms_send.at[sweep, distance - 1],
            recv_sem=terms_recv.at[sweep, distance - 1],
            device_id=member(ahead(distance)),
        )

    def shared_copy(sweep, distance, owner):
        return pltpu.make_async_remote_copy(
            src_ref=shared_low.at[sweep, own_slice(owner)],
            dst_ref=shared_low.at[sweep, own_slice(owner)],
            send_sem=shared_send.at[sweep, distance - 1],
            recv_sem=shared_recv.at[sweep, distance - 1],
            device_id=member(ahead(distance)),
        )

    def onward_copy(sweep):
        return pltpu.make_async_remote_copy(
            src_ref=current.at[sweep],
            dst_ref=previous.at[sweep],
            send_sem=chain_send.at[sweep],
            recv_sem=chain_recv.at[sweep],
            device_id={"chain": lax.rem(week + 1, weeks)},
        )

    def backward_copy(sweep):
        return pltpu.make_async_remote_copy(
            src_ref=current.at[sweep],
            dst_ref=later.at[sweep],
            send_sem=chain_send.at[SWEEPS + sweep],
            recv_sem=chain_recv.at[SWEEPS + sweep],
            device_id={"chain": lax.rem(week + weeks - 1, weeks)},
        )

    def gather_start(sweep, index):
        for distance in range(1, parts):
            gather_copy(sweep, distance, index).start()

    for index in range(chunks):
        gather_start(0, index)

    row_count = seen_ref.shape[1]
    seen[...] = jnp.transpose(jnp.broadcast_to(seen_ref[...], (128, row_count)))
    week_rhs[...] = jnp.transpose(week_rhs_ref[...])
    high, low = split_two(week_inverse_ref[...])
    inverse_high[...] = high
    inverse_low[...] = low
    walk = walk_ref[...]

    def solve_shared(value):
        value_high, value_low = split_two(value)
        first = jnp.dot(
            jnp.concatenate([value_high, value_low], axis=0),
            inverse_high[...],
            preferred_element_type=F32,
        )
        second = jnp.dot(value_high, inverse_low[...], preferred_element_type=F32)
        return first[:piece] + (first[piece:] + second)

    def add_columns(slot, start, width, block, begin):
        @pl.loop(0, rows // tile)
        def _(index):
            span = pl.ds(pl.multiple_of(index * tile, tile), tile)
            product = jnp.dot(
                inverse[slot, span, start : start + width], block, preferred_element_type=F32
            )
            if begin:
                coords[span, :] = product
            else:
                coords[span, :] += product

    for load in loads:
        load.wait()
    coords_out = pltpu.make_async_copy(coords, coords_hbm, local_sem.at[0])
    for sweep in range(SWEEPS):
        if sweep == 0:
            own = rhs
        else:
            own = residual
            for index in range(chunks):
                span = slice(index * chunk, (index + 1) * chunk)
                product = lax.dot_general(
                    coupling[span, :], shared_low[sweep - 1], NT, preferred_element_type=F32
                )
                residual[span, :] = (rhs[span, :].astype(F32) - product).astype(BF16)
                gather_start(sweep, index)
        add_columns(0, 0, rows, own[...], True)
        for index in range(chunks):
            span = slice(index * chunk, (index + 1) * chunk)
            for distance in range(1, parts):
                gather_copy(sweep, distance, index).wait_recv()
                add_columns(
                    distance, index * chunk, chunk, arrived[sweep, distance - 1, span, :], False
                )

        @pl.loop(0, rows // tile)
        def _(index):
            span = pl.ds(pl.multiple_of(index * tile, tile), tile)
            value = coords[span, :] * seen[span, 0:1]
            coords_low[span, :] = value.astype(BF16)
            if sweep == SWEEPS - 1:
                coords[span, :] = value

        if sweep == SWEEPS - 1:
            coords_out.start()
        terms[...] = lax.dot_general(
            coords_low[...], coupling[...], TN, preferred_element_type=F32
        )
        terms_low[sweep] = terms[...].astype(BF16)
        for distance in range(1, team):
            terms_copy(sweep, distance).start()

        right = week_rhs[own_slice(rank), :] - terms[own_slice(rank), :]
        if sweep > 0:
            @pl.when(not_last)
            def _():
                backward_copy(sweep - 1).wait_recv()

            @pl.when(jnp.logical_not(not_last))
            def _():
                later[sweep - 1] = jnp.zeros(later.shape[1:], F32)

            right += walk * later[sweep - 1]
        for distance in range(1, team):
            terms_copy(sweep, distance).wait_recv()
            right -= terms_in[sweep, distance - 1].astype(F32)
        current[sweep] = solve_shared(right)

        @pl.when(not_first)
        def _():
            onward_copy(sweep).wait_recv()
            current[sweep] += solve_shared(walk * previous[sweep])

        @pl.when(not_last)
        def _():
            onward_copy(sweep).start()

        shared_low[sweep, own_slice(rank), :] = current[sweep].astype(BF16)
        for distance in range(1, team):
            shared_copy(sweep, distance, rank).start()
        if sweep < SWEEPS - 1:
            @pl.when(not_first)
            def _():
                backward_copy(sweep).start()

        for distance in range(1, team):
            shared_copy(sweep, distance, behind(distance)).wait_recv()

    shared_ref[...] = shared_low[SWEEPS - 1].astype(F32)

    for sweep in range(SWEEPS):
        for distance in range(1, parts):
            for index in range(chunks):
                gather_copy(sweep, distance, index).wait_send()
        for distance in range(1, team):
            terms_copy(sweep, distance).wait_send()
            shared_copy(sweep, distance, rank).wait_send()

        @pl.when(not_last)
        def _():
            onward_copy(sweep).wait_send()

        if sweep < SWEEPS - 1:
            @pl.when(not_first)
            def _():
                backward_copy(sweep).wait_send()

    coords_out.wait()


def whole_step(size, limit):
    step = min(size, limit)
    while size % step:
        step -= 16
    return step


def shards(
    mesh_shape,
    block_inverse,
    coupling,
    data_rhs,
    station_seen,
    shared_inverse,
    walk_weight,
    shared_rhs,
):
    weeks, groups, parts = (mesh_shape[axis] for axis in ("chain", "tech", "blk"))
    team = groups * parts
    rows, samples = data_rhs.shape[2:]
    width = shared_inverse.shape[1]
    piece = samples // team
    chunk = whole_step(rows, 512)
    tile = whole_step(rows, 512)
    chunks = rows // chunk
    seen_row = jnp.repeat(station_seen[0, 0].astype(F32), 3)[None, :]
    vmem = pl.BlockSpec(memory_space=pltpu.VMEM)
    anywhere = pl.BlockSpec(memory_space=pl.ANY)
    dma = pltpu.SemaphoreType.DMA
    others = max(parts - 1, 1)
    coords, shared = pl.pallas_call(
        functools.partial(kernel, weeks, groups, parts, chunk, tile),
        out_shape=(
            jax.ShapeDtypeStruct((rows, samples), F32),
            jax.ShapeDtypeStruct((samples, width), F32),
        ),
        in_specs=[anywhere] * 3 + [vmem] * 4,
        out_specs=(anywhere, vmem),
        scratch_shapes=[
            pltpu.VMEM((parts, rows, rows), BF16),
            pltpu.VMEM((rows, width), BF16),
            pltpu.VMEM((rows, samples), BF16),
            pltpu.VMEM((rows, samples), BF16),
            pltpu.VMEM((SWEEPS, others, rows, samples), BF16),
            pltpu.VMEM((rows, samples), F32),
            pltpu.VMEM((rows, samples), BF16),
            pltpu.VMEM((rows, 128), F32),
            pltpu.VMEM((samples, width), F32),
            pltpu.VMEM((width, width), BF16),
            pltpu.VMEM((width, width), BF16),
            pltpu.VMEM((samples, width), F32),
            pltpu.VMEM((SWEEPS, samples, width), BF16),
            pltpu.VMEM((SWEEPS, team - 1, piece, width), BF16),
            pltpu.VMEM((SWEEPS, samples, width), BF16),
            pltpu.VMEM((SWEEPS, piece, width), F32),
            pltpu.VMEM((SWEEPS, piece, width), F32),
            pltpu.VMEM((SWEEPS, piece, width), F32),
            dma((2 + parts,)),
            dma((SWEEPS, others, chunks)),
            dma((SWEEPS, others, chunks)),
            dma((SWEEPS, team - 1)),
            dma((SWEEPS, team - 1)),
            dma((SWEEPS, team - 1)),
            dma((SWEEPS, team - 1)),
            dma((2 * SWEEPS,)),
            dma((2 * SWEEPS,)),
        ],
        compiler_params=pltpu.CompilerParams(
            collective_id=0, has_side_effects=True, vmem_limit_bytes=48 * 2**20
        ),
        cost_estimate=pl.CostEstimate(
            flops=2 * SWEEPS * rows * samples * (rows * parts + 2 * width),
            bytes_accessed=2 * rows * (rows * parts + width + samples) + 4 * rows * samples,
            transcendentals=0,
        ),
    )(
        block_inverse[0, 0],
        coupling[0, 0],
        data_rhs[0, 0],
        seen_row,
        shared_inverse[0],
        walk_weight[None, :],
        shared_rhs[0],
    )
    return coords[None, None], shared.T[None]


def solution(mesh):
    in_specs = (
        P("tech", "chain", "blk", None),
        P("tech", "chain", "blk", None),
        P("tech", "chain", "blk", None),
        P("tech", "chain", "blk"),
        P("chain", None, None),
        P(),
        P("chain", None, None),
    )
    out_specs = (P("tech", "chain", "blk", None), P("chain", None, None))
    return jax.shard_map(
        functools.partial(shards, dict(mesh.shape)),
        mesh=mesh,
        in_specs=in_specs,
        out_specs=out_specs,
        check_vma=False,
    )
```

```python
import functools

import jax
import jax.numpy as jnp
from jax import lax
from jax.experimental import pallas as pl
from jax.experimental.pallas import tpu as pltpu
from jax.sharding import PartitionSpec as P

SWEEPS = 2
F32 = jnp.float32
BF16 = jnp.bfloat16
NT = (((1,), (1,)), ((), ()))
TN = (((0,), (0,)), ((), ()))


def split_two(value):
    high = value.astype(BF16)
    return high, (value - high.astype(F32)).astype(BF16)


def kernel(
    weeks,
    groups,
    parts,
    halves,
    chunk,
    tile,
    inverse_hbm,
    coupling_hbm,
    rhs_hbm,
    seen_ref,
    week_inverse_hbm,
    walk_ref,
    week_rhs_hbm,
    coords_hbm,
    shared_ref,
    inverse,
    coupling,
    rhs,
    residual,
    arrived,
    coords,
    coords_low,
    seen,
    week_inverse_in,
    week_rhs_in,
    week_rhs,
    inverse_high,
    inverse_low,
    terms,
    terms_low,
    terms_in,
    shared_low,
    current,
    previous,
    later,
    local_sem,
    gather_send,
    gather_recv,
    terms_send,
    terms_recv,
    shared_send,
    shared_recv,
    chain_send,
    chain_recv,
):
    week = lax.axis_index("chain")
    group = lax.axis_index("tech")
    part = lax.axis_index("blk")
    team = groups * parts
    rank = group * parts + part
    rows = rhs.shape[0]
    piece = current.shape[2]
    half_samples = piece * team
    chunks = rows // chunk
    not_first = week > 0
    not_last = week < weeks - 1

    def member(number):
        return {"tech": number // parts, "blk": lax.rem(number, parts)}

    def ahead(distance):
        return lax.rem(rank + distance, team)

    def behind(distance):
        return lax.rem(rank + team - distance, team)

    def own_slice(half, number):
        return pl.ds(pl.multiple_of(half * half_samples + number * piece, piece), piece)

    def half_slice(half):
        return slice(half * half_samples, (half + 1) * half_samples)

    loads = []
    loads.append(pltpu.make_async_copy(rhs_hbm, rhs, local_sem.at[0]))
    for slot in range(parts):
        column = pl.multiple_of(lax.rem(part + parts - slot, parts) * rows, 128)
        loads.append(
            pltpu.make_async_copy(
                inverse_hbm.at[:, pl.ds(column, rows)], inverse.at[slot], local_sem.at[1 + slot]
            )
        )
    loads.append(pltpu.make_async_copy(coupling_hbm, coupling, local_sem.at[1 + parts]))
    loads.append(
        pltpu.make_async_copy(week_inverse_hbm, week_inverse_in, local_sem.at[2 + parts])
    )
    loads.append(pltpu.make_async_copy(week_rhs_hbm, week_rhs_in, local_sem.at[3 + parts]))
    for load in loads:
        load.start()

    barrier = pltpu.get_barrier_semaphore()
    for distance in range(1, team):
        pl.semaphore_signal(barrier, inc=1, device_id=member(ahead(distance)))

    @pl.when(not_first)
    def _():
        pl.semaphore_signal(barrier, inc=1, device_id={"chain": week - 1})

    @pl.when(not_last)
    def _():
        pl.semaphore_signal(barrier, inc=1, device_id={"chain": week + 1})

    pl.semaphore_wait(
        barrier, team - 1 + not_first.astype(jnp.int32) + not_last.astype(jnp.int32)
    )

    def gather_copy(sweep, half, distance, index):
        span = pl.ds(index * chunk, chunk)
        if sweep == 0:
            source = rhs_hbm.at[span, pl.ds(half * half_samples, half_samples)]
        else:
            source = residual.at[half, span]
        return pltpu.make_async_remote_copy(
            src_ref=source,
            dst_ref=arrived.at[sweep, half, distance - 1, span],
            send_sem=gather_send.at[sweep, half, distance - 1, index],
            recv_sem=gather_recv.at[sweep, half, distance - 1, index],
            device_id={"blk": lax.rem(part + distance, parts)},
        )

    def terms_copy(sweep, half, distance):
        return pltpu.make_async_remote_copy(
            src_ref=terms_low.at[sweep, own_slice(half, ahead(distance))],
            dst_ref=terms_in.at[sweep, half, distance - 1],
            send_sem=terms_send.at[sweep, half, distance - 1],
            recv_sem=terms_recv.at[sweep, half, distance - 1],
            device_id=member(ahead(distance)),
        )

    def shared_copy(sweep, half, distance, owner):
        return pltpu.make_async_remote_copy(
            src_ref=shared_low.at[sweep, own_slice(half, owner)],
            dst_ref=shared_low.at[sweep, own_slice(half, owner)],
            send_sem=shared_send.at[sweep, half, distance - 1],
            recv_sem=shared_recv.at[sweep, half, distance - 1],
            device_id=member(ahead(distance)),
        )

    def onward_copy(sweep, half):
        return pltpu.make_async_remote_copy(
            src_ref=current.at[sweep, half],
            dst_ref=previous.at[sweep, half],
            send_sem=chain_send.at[sweep, half],
            recv_sem=chain_recv.at[sweep, half],
            device_id={"chain": lax.rem(week + 1, weeks)},
        )

    def backward_copy(sweep, half):
        return pltpu.make_async_remote_copy(
            src_ref=current.at[sweep, half],
            dst_ref=later.at[sweep, half],
            send_sem=chain_send.at[SWEEPS + sweep, half],
            recv_sem=chain_recv.at[SWEEPS + sweep, half],
            device_id={"chain": lax.rem(week + weeks - 1, weeks)},
        )

    def gather_start(sweep, half, index):
        for distance in range(1, parts):
            gather_copy(sweep, half, distance, index).start()

    for half in range(halves):
        for index in range(chunks):
            gather_start(0, half, index)

    row_count = seen_ref.shape[1]
    seen[...] = jnp.transpose(jnp.broadcast_to(seen_ref[...], (128, row_count)))
    for load in loads:
        load.wait()
    week_rhs[...] = jnp.transpose(week_rhs_in[...])
    high, low = split_two(week_inverse_in[...])
    inverse_high[...] = high
    inverse_low[...] = low
    walk = walk_ref[...]

    def solve_shared(value):
        value_high, value_low = split_two(value)
        first = jnp.dot(
            jnp.concatenate([value_high, value_low], axis=0),
            inverse_high[...],
            preferred_element_type=F32,
        )
        second = jnp.dot(value_high, inverse_low[...], preferred_element_type=F32)
        return first[:piece] + (first[piece:] + second)

    def add_columns(half, slot, start, width, block, begin):
        @pl.loop(0, rows // tile)
        def _(index):
            span = pl.ds(pl.multiple_of(index * tile, tile), tile)
            product = jnp.dot(
                inverse[slot, span, start : start + width], block, preferred_element_type=F32
            )
            if begin:
                coords[span, half_slice(half)] = product
            else:
                coords[span, half_slice(half)] += product

    def make_residual(sweep, half):
        for distance in range(1, team):
            shared_copy(sweep - 1, half, distance, behind(distance)).wait_recv()
        for index in range(chunks):
            span = slice(index * chunk, (index + 1) * chunk)
            product = lax.dot_general(
                coupling[span, :],
                shared_low[sweep - 1, half_slice(half), :],
                NT,
                preferred_element_type=F32,
            )
            residual[half, span, :] = (
                rhs[span, half_slice(half)].astype(F32) - product
            ).astype(BF16)
            gather_start(sweep, half, index)

    def make_terms(sweep, half):
        own = rhs[:, half_slice(half)] if sweep == 0 else residual[half]
        add_columns(half, 0, 0, rows, own, True)
        for index in range(chunks):
            span = slice(index * chunk, (index + 1) * chunk)
            for distance in range(1, parts):
                gather_copy(sweep, half, distance, index).wait_recv()
                block = arrived[sweep, half, distance - 1, span, :]
                add_columns(half, distance, index * chunk, chunk, block, False)

        @pl.loop(0, rows // tile)
        def _(index):
            span = pl.ds(pl.multiple_of(index * tile, tile), tile)
            value = coords[span, half_slice(half)] * seen[span, 0:1]
            coords_low[span, :] = value.astype(BF16)
            if sweep == SWEEPS - 1:
                coords[span, half_slice(half)] = value

        product = lax.dot_general(
            coords_low[...], coupling[...], TN, preferred_element_type=F32
        )
        terms[half_slice(half), :] = product
        terms_low[sweep, half_slice(half), :] = product.astype(BF16)
        for distance in range(1, team):
            terms_copy(sweep, half, distance).start()

    def make_shared(sweep, half):
        own = own_slice(half, rank)
        right = week_rhs[own, :] - terms[own, :]
        if sweep > 0:
            @pl.when(not_last)
            def _():
                backward_copy(sweep - 1, half).wait_recv()

            @pl.when(jnp.logical_not(not_last))
            def _():
                later[sweep - 1, half] = jnp.zeros(later.shape[2:], F32)

            right += walk * later[sweep - 1, half]
        for distance in range(1, team):
            terms_copy(sweep, half, distance).wait_recv()
            right -= terms_in[sweep, half, distance - 1].astype(F32)
        current[sweep, half] = solve_shared(right)

        @pl.when(not_first)
        def _():
            onward_copy(sweep, half).wait_recv()
            current[sweep, half] += solve_shared(walk * previous[sweep, half])

        @pl.when(not_last)
        def _():
            onward_copy(sweep, half).start()

        shared_low[sweep, own, :] = current[sweep, half].astype(BF16)
        for distance in range(1, team):
            shared_copy(sweep, half, distance, rank).start()
        if sweep < SWEEPS - 1:
            @pl.when(not_first)
            def _():
                backward_copy(sweep, half).start()

    coords_out = pltpu.make_async_copy(coords, coords_hbm, local_sem.at[0])

    for sweep in range(SWEEPS):
        for half in range(halves):
            make_terms(sweep, half)
            if sweep == SWEEPS - 1 and half == halves - 1:
                coords_out.start()
            if sweep < SWEEPS - 1 and half > 0:
                make_residual(sweep + 1, half - 1)
            make_shared(sweep, half)
        if sweep < SWEEPS - 1:
            make_residual(sweep + 1, halves - 1)
        else:
            for half in range(halves):
                for distance in range(1, team):
                    shared_copy(sweep, half, distance, behind(distance)).wait_recv()

    shared_ref[...] = shared_low[SWEEPS - 1].astype(F32)

    for sweep in range(SWEEPS):
        for half in range(halves):
            for distance in range(1, parts):
                for index in range(chunks):
                    gather_copy(sweep, half, distance, index).wait_send()
            for distance in range(1, team):
                terms_copy(sweep, half, distance).wait_send()
                shared_copy(sweep, half, distance, rank).wait_send()

            @pl.when(not_last)
            def _():
                onward_copy(sweep, half).wait_send()

            if sweep < SWEEPS - 1:
                @pl.when(not_first)
                def _():
                    backward_copy(sweep, half).wait_send()

    coords_out.wait()


def whole_step(size, limit):
    step = min(size, limit)
    while size % step:
        step -= 16
    return step


def shards(
    mesh_shape,
    block_inverse,
    coupling,
    data_rhs,
    station_seen,
    shared_inverse,
    walk_weight,
    shared_rhs,
):
    weeks, groups, parts = (mesh_shape[axis] for axis in ("chain", "tech", "blk"))
    team = groups * parts
    rows, samples = data_rhs.shape[2:]
    width = shared_inverse.shape[1]
    halves = 2 if samples % (2 * max(128, 16 * team)) == 0 else 1
    half_samples = samples // halves
    piece = half_samples // team
    chunk = whole_step(rows, 512)
    tile = whole_step(rows, 512)
    chunks = rows // chunk
    seen_row = jnp.repeat(station_seen[0, 0].astype(F32), 3)[None, :]
    vmem = pl.BlockSpec(memory_space=pltpu.VMEM)
    anywhere = pl.BlockSpec(memory_space=pl.ANY)
    dma = pltpu.SemaphoreType.DMA
    others = max(parts - 1, 1)
    coords, shared = pl.pallas_call(
        functools.partial(kernel, weeks, groups, parts, halves, chunk, tile),
        out_shape=(
            jax.ShapeDtypeStruct((rows, samples), F32),
            jax.ShapeDtypeStruct((samples, width), F32),
        ),
        in_specs=[anywhere] * 3 + [vmem, anywhere, vmem, anywhere],
        out_specs=(anywhere, vmem),
        scratch_shapes=[
            pltpu.VMEM((parts, rows, rows), BF16),
            pltpu.VMEM((rows, width), BF16),
            pltpu.VMEM((rows, samples), BF16),
            pltpu.VMEM((halves, rows, half_samples), BF16),
            pltpu.VMEM((SWEEPS, halves, others, rows, half_samples), BF16),
            pltpu.VMEM((rows, samples), F32),
            pltpu.VMEM((rows, half_samples), BF16),
            pltpu.VMEM((rows, 128), F32),
            pltpu.VMEM((width, width), F32),
            pltpu.VMEM((width, samples), F32),
            pltpu.VMEM((samples, width), F32),
            pltpu.VMEM((width, width), BF16),
            pltpu.VMEM((width, width), BF16),
            pltpu.VMEM((samples, width), F32),
            pltpu.VMEM((SWEEPS, samples, width), BF16),
            pltpu.VMEM((SWEEPS, halves, team - 1, piece, width), BF16),
            pltpu.VMEM((SWEEPS, samples, width), BF16),
            pltpu.VMEM((SWEEPS, halves, piece, width), F32),
            pltpu.VMEM((SWEEPS, halves, piece, width), F32),
            pltpu.VMEM((SWEEPS, halves, piece, width), F32),
            dma((4 + parts,)),
            dma((SWEEPS, halves, others, chunks)),
            dma((SWEEPS, halves, others, chunks)),
            dma((SWEEPS, halves, team - 1)),
            dma((SWEEPS, halves, team - 1)),
            dma((SWEEPS, halves, team - 1)),
            dma((SWEEPS, halves, team - 1)),
            dma((2 * SWEEPS, halves)),
            dma((2 * SWEEPS, halves)),
        ],
        compiler_params=pltpu.CompilerParams(
            collective_id=0, has_side_effects=True, vmem_limit_bytes=60 * 2**20
        ),
        cost_estimate=pl.CostEstimate(
            flops=2 * SWEEPS * rows * samples * (rows * parts + 2 * width),
            bytes_accessed=2 * rows * (rows * parts + width + samples) + 4 * rows * samples,
            transcendentals=0,
        ),
    )(
        block_inverse[0, 0],
        coupling[0, 0],
        data_rhs[0, 0],
        seen_row,
        shared_inverse[0],
        walk_weight[None, :],
        shared_rhs[0],
    )
    return coords[None, None], shared.T[None]


def solution(mesh):
    in_specs = (
        P("tech", "chain", "blk", None),
        P("tech", "chain", "blk", None),
        P("tech", "chain", "blk", None),
        P("tech", "chain", "blk"),
        P("chain", None, None),
        P(),
        P("chain", None, None),
    )
    out_specs = (P("tech", "chain", "blk", None), P("chain", None, None))
    return jax.shard_map(
        functools.partial(shards, dict(mesh.shape)),
        mesh=mesh,
        in_specs=in_specs,
        out_specs=out_specs,
        check_vma=False,
    )
```

```python
import functools

import jax
import jax.numpy as jnp
from jax import lax
from jax.experimental import pallas as pl
from jax.experimental.pallas import tpu as pltpu
from jax.sharding import PartitionSpec as P

SWEEPS = 2
HALVES = 1
F32 = jnp.float32
BF16 = jnp.bfloat16
NT = (((1,), (1,)), ((), ()))
TN = (((0,), (0,)), ((), ()))


def split_two(value):
    high = value.astype(BF16)
    return high, (value - high.astype(F32)).astype(BF16)


def kernel(
    weeks,
    groups,
    parts,
    halves,
    chunk,
    tile,
    inverse_hbm,
    coupling_hbm,
    rhs_hbm,
    seen_ref,
    week_inverse_hbm,
    walk_ref,
    week_rhs_hbm,
    coords_hbm,
    shared_ref,
    inverse,
    coupling,
    rhs,
    residual,
    arrived,
    coords,
    coords_low,
    seen,
    week_inverse_in,
    week_rhs_in,
    week_rhs,
    inverse_high,
    inverse_low,
    terms,
    terms_low,
    terms_in,
    shared_low,
    current,
    previous,
    later,
    local_sem,
    gather_send,
    gather_recv,
    terms_send,
    terms_recv,
    shared_send,
    shared_recv,
    chain_send,
    chain_recv,
):
    week = lax.axis_index("chain")
    group = lax.axis_index("tech")
    part = lax.axis_index("blk")
    team = groups * parts
    rank = group * parts + part
    rows = rhs.shape[0]
    piece = current.shape[2]
    half_samples = piece * team
    chunks = rows // chunk
    not_first = week > 0
    not_last = week < weeks - 1

    def member(number):
        return {"tech": number // parts, "blk": lax.rem(number, parts)}

    def ahead(distance):
        return lax.rem(rank + distance, team)

    def behind(distance):
        return lax.rem(rank + team - distance, team)

    def own_slice(half, number):
        return pl.ds(pl.multiple_of(half * half_samples + number * piece, piece), piece)

    def half_slice(half):
        return slice(half * half_samples, (half + 1) * half_samples)

    loads = []
    loads.append(pltpu.make_async_copy(rhs_hbm, rhs, local_sem.at[0]))
    for slot in range(parts):
        column = pl.multiple_of(lax.rem(part + parts - slot, parts) * rows, 128)
        loads.append(
            pltpu.make_async_copy(
                inverse_hbm.at[:, pl.ds(column, rows)], inverse.at[slot], local_sem.at[1 + slot]
            )
        )
    loads.append(pltpu.make_async_copy(coupling_hbm, coupling, local_sem.at[1 + parts]))
    loads.append(
        pltpu.make_async_copy(week_inverse_hbm, week_inverse_in, local_sem.at[2 + parts])
    )
    loads.append(pltpu.make_async_copy(week_rhs_hbm, week_rhs_in, local_sem.at[3 + parts]))
    for load in loads:
        load.start()

    barrier = pltpu.get_barrier_semaphore()
    for distance in range(1, team):
        pl.semaphore_signal(barrier, inc=1, device_id=member(ahead(distance)))

    @pl.when(not_first)
    def _():
        pl.semaphore_signal(barrier, inc=1, device_id={"chain": week - 1})

    @pl.when(not_last)
    def _():
        pl.semaphore_signal(barrier, inc=1, device_id={"chain": week + 1})

    pl.semaphore_wait(
        barrier, team - 1 + not_first.astype(jnp.int32) + not_last.astype(jnp.int32)
    )

    def gather_copy(sweep, half, distance, index):
        span = pl.ds(index * chunk, chunk)
        if sweep == 0:
            source = rhs_hbm.at[span, pl.ds(half * half_samples, half_samples)]
        else:
            source = residual.at[half, span]
        return pltpu.make_async_remote_copy(
            src_ref=source,
            dst_ref=arrived.at[sweep, half, distance - 1, span],
            send_sem=gather_send.at[sweep, half, distance - 1, index],
            recv_sem=gather_recv.at[sweep, half, distance - 1, index],
            device_id={"blk": lax.rem(part + distance, parts)},
        )

    def terms_copy(sweep, half, distance):
        return pltpu.make_async_remote_copy(
            src_ref=terms_low.at[sweep, own_slice(half, ahead(distance))],
            dst_ref=terms_in.at[sweep, half, distance - 1],
            send_sem=terms_send.at[sweep, half, distance - 1],
            recv_sem=terms_recv.at[sweep, half, distance - 1],
            device_id=member(ahead(distance)),
        )

    def shared_copy(sweep, half, distance, owner):
        return pltpu.make_async_remote_copy(
            src_ref=shared_low.at[sweep, own_slice(half, owner)],
            dst_ref=shared_low.at[sweep, own_slice(half, owner)],
            send_sem=shared_send.at[sweep, half, distance - 1],
            recv_sem=shared_recv.at[sweep, half, distance - 1],
            device_id=member(ahead(distance)),
        )

    def onward_copy(sweep, half):
        return pltpu.make_async_remote_copy(
            src_ref=current.at[sweep, half],
            dst_ref=previous.at[sweep, half],
            send_sem=chain_send.at[sweep, half],
            recv_sem=chain_recv.at[sweep, half],
            device_id={"chain": lax.rem(week + 1, weeks)},
        )

    def backward_copy(sweep, half):
        return pltpu.make_async_remote_copy(
            src_ref=current.at[sweep, half],
            dst_ref=later.at[sweep, half],
            send_sem=chain_send.at[SWEEPS + sweep, half],
            recv_sem=chain_recv.at[SWEEPS + sweep, half],
            device_id={"chain": lax.rem(week + weeks - 1, weeks)},
        )

    def gather_start(sweep, half, index):
        for distance in range(1, parts):
            gather_copy(sweep, half, distance, index).start()

    for half in range(halves):
        for index in range(chunks):
            gather_start(0, half, index)

    stations = seen_ref.shape[1]
    per_station = rows // stations

    @pl.loop(0, rows // tile)
    def _(index):
        start = pl.multiple_of(index * tile, tile)
        row = start + lax.broadcasted_iota(jnp.int32, (tile, stations), 0)
        offset = row - per_station * lax.broadcasted_iota(jnp.int32, (tile, stations), 1)
        inside = jnp.logical_and(offset >= 0, offset < per_station)
        picked = jnp.where(inside, seen_ref[...].astype(F32), 0.0)
        column = jnp.sum(picked, axis=1, keepdims=True)
        seen[pl.ds(start, tile), :] = jnp.broadcast_to(column, (tile, 128))

    for load in loads:
        load.wait()
    week_rhs[...] = jnp.transpose(week_rhs_in[...])
    high, low = split_two(week_inverse_in[...])
    inverse_high[...] = high
    inverse_low[...] = low
    walk = walk_ref[...]

    def solve_shared(value):
        value_high, value_low = split_two(value)
        first = jnp.dot(
            jnp.concatenate([value_high, value_low], axis=0),
            inverse_high[...],
            preferred_element_type=F32,
        )
        second = jnp.dot(value_high, inverse_low[...], preferred_element_type=F32)
        return first[:piece] + (first[piece:] + second)

    def add_columns(half, slot, start, width, block, begin):
        @pl.loop(0, rows // tile)
        def _(index):
            span = pl.ds(pl.multiple_of(index * tile, tile), tile)
            product = jnp.dot(
                inverse[slot, span, start : start + width], block, preferred_element_type=F32
            )
            if begin:
                coords[span, half_slice(half)] = product
            else:
                coords[span, half_slice(half)] += product

    def make_residual(sweep, half):
        for distance in range(1, team):
            shared_copy(sweep - 1, half, distance, behind(distance)).wait_recv()
        for index in range(chunks):
            span = slice(index * chunk, (index + 1) * chunk)
            product = lax.dot_general(
                coupling[span, :],
                shared_low[sweep - 1, half_slice(half), :],
                NT,
                preferred_element_type=F32,
            )
            residual[half, span, :] = (
                rhs[span, half_slice(half)].astype(F32) - product
            ).astype(BF16)
            gather_start(sweep, half, index)

    def make_terms(sweep, half):
        own = rhs[:, half_slice(half)] if sweep == 0 else residual[half]
        add_columns(half, 0, 0, rows, own, True)
        for index in range(chunks):
            span = slice(index * chunk, (index + 1) * chunk)
            for distance in range(1, parts):
                gather_copy(sweep, half, distance, index).wait_recv()
                block = arrived[sweep, half, distance - 1, span, :]
                add_columns(half, distance, index * chunk, chunk, block, False)

        @pl.loop(0, rows // tile)
        def _(index):
            span = pl.ds(pl.multiple_of(index * tile, tile), tile)
            value = coords[span, half_slice(half)] * seen[span, 0:1]
            coords_low[span, :] = value.astype(BF16)
            if sweep == SWEEPS - 1:
                coords[span, half_slice(half)] = value

        product = lax.dot_general(
            coords_low[...], coupling[...], TN, preferred_element_type=F32
        )
        terms[half_slice(half), :] = product
        terms_low[sweep, half_slice(half), :] = product.astype(BF16)
        for distance in range(1, team):
            terms_copy(sweep, half, distance).start()

    def make_shared(sweep, half):
        own = own_slice(half, rank)
        right = week_rhs[own, :] - terms[own, :]
        if sweep > 0:
            @pl.when(not_last)
            def _():
                backward_copy(sweep - 1, half).wait_recv()

            @pl.when(jnp.logical_not(not_last))
            def _():
                later[sweep - 1, half] = jnp.zeros(later.shape[2:], F32)

            right += walk * later[sweep - 1, half]
        for distance in range(1, team):
            terms_copy(sweep, half, distance).wait_recv()
            right -= terms_in[sweep, half, distance - 1].astype(F32)
        current[sweep, half] = solve_shared(right)

        @pl.when(not_first)
        def _():
            onward_copy(sweep, half).wait_recv()
            current[sweep, half] += solve_shared(walk * previous[sweep, half])

        @pl.when(not_last)
        def _():
            onward_copy(sweep, half).start()

        shared_low[sweep, own, :] = current[sweep, half].astype(BF16)
        for distance in range(1, team):
            shared_copy(sweep, half, distance, rank).start()
        if sweep < SWEEPS - 1:
            @pl.when(not_first)
            def _():
                backward_copy(sweep, half).start()

    coords_out = pltpu.make_async_copy(coords, coords_hbm, local_sem.at[0])

    for sweep in range(SWEEPS):
        for half in range(halves):
            make_terms(sweep, half)
            if sweep == SWEEPS - 1 and half == halves - 1:
                coords_out.start()
            if sweep < SWEEPS - 1 and half > 0:
                make_residual(sweep + 1, half - 1)
            make_shared(sweep, half)
        if sweep < SWEEPS - 1:
            make_residual(sweep + 1, halves - 1)
        else:
            for half in range(halves):
                for distance in range(1, team):
                    shared_copy(sweep, half, distance, behind(distance)).wait_recv()

    shared_ref[...] = shared_low[SWEEPS - 1].astype(F32)

    for sweep in range(SWEEPS):
        for half in range(halves):
            for distance in range(1, parts):
                for index in range(chunks):
                    gather_copy(sweep, half, distance, index).wait_send()
            for distance in range(1, team):
                terms_copy(sweep, half, distance).wait_send()
                shared_copy(sweep, half, distance, rank).wait_send()

            @pl.when(not_last)
            def _():
                onward_copy(sweep, half).wait_send()

            if sweep < SWEEPS - 1:
                @pl.when(not_first)
                def _():
                    backward_copy(sweep, half).wait_send()

    coords_out.wait()


def whole_step(size, limit):
    step = min(size, limit)
    while size % step:
        step -= 16
    return step


def shards(
    mesh_shape,
    block_inverse,
    coupling,
    data_rhs,
    station_seen,
    shared_inverse,
    walk_weight,
    shared_rhs,
):
    weeks, groups, parts = (mesh_shape[axis] for axis in ("chain", "tech", "blk"))
    team = groups * parts
    rows, samples = data_rhs.shape[2:]
    width = shared_inverse.shape[1]
    halves = HALVES
    half_samples = samples // halves
    piece = half_samples // team
    chunk = whole_step(rows, 512)
    tile = whole_step(rows, 512)
    chunks = rows // chunk
    vmem = pl.BlockSpec(memory_space=pltpu.VMEM)
    anywhere = pl.BlockSpec(memory_space=pl.ANY)
    dma = pltpu.SemaphoreType.DMA
    others = max(parts - 1, 1)
    coords, shared = pl.pallas_call(
        functools.partial(kernel, weeks, groups, parts, halves, chunk, tile),
        out_shape=(
            jax.ShapeDtypeStruct((rows, samples), F32),
            jax.ShapeDtypeStruct((samples, width), F32),
        ),
        in_specs=[anywhere] * 3 + [vmem, anywhere, vmem, anywhere],
        out_specs=(anywhere, vmem),
        scratch_shapes=[
            pltpu.VMEM((parts, rows, rows), BF16),
            pltpu.VMEM((rows, width), BF16),
            pltpu.VMEM((rows, samples), BF16),
            pltpu.VMEM((halves, rows, half_samples), BF16),
            pltpu.VMEM((SWEEPS, halves, others, rows, half_samples), BF16),
            pltpu.VMEM((rows, samples), F32),
            pltpu.VMEM((rows, half_samples), BF16),
            pltpu.VMEM((rows, 128), F32),
            pltpu.VMEM((width, width), F32),
            pltpu.VMEM((width, samples), F32),
            pltpu.VMEM((samples, width), F32),
            pltpu.VMEM((width, width), BF16),
            pltpu.VMEM((width, width), BF16),
            pltpu.VMEM((samples, width), F32),
            pltpu.VMEM((SWEEPS, samples, width), BF16),
            pltpu.VMEM((SWEEPS, halves, team - 1, piece, width), BF16),
            pltpu.VMEM((SWEEPS, samples, width), BF16),
            pltpu.VMEM((SWEEPS, halves, piece, width), F32),
            pltpu.VMEM((SWEEPS, halves, piece, width), F32),
            pltpu.VMEM((SWEEPS, halves, piece, width), F32),
            dma((4 + parts,)),
            dma((SWEEPS, halves, others, chunks)),
            dma((SWEEPS, halves, others, chunks)),
            dma((SWEEPS, halves, team - 1)),
            dma((SWEEPS, halves, team - 1)),
            dma((SWEEPS, halves, team - 1)),
            dma((SWEEPS, halves, team - 1)),
            dma((2 * SWEEPS, halves)),
            dma((2 * SWEEPS, halves)),
        ],
        compiler_params=pltpu.CompilerParams(
            collective_id=0, has_side_effects=True, vmem_limit_bytes=60 * 2**20
        ),
        cost_estimate=pl.CostEstimate(
            flops=2 * SWEEPS * rows * samples * (rows * parts + 2 * width),
            bytes_accessed=2 * rows * (rows * parts + width + samples) + 4 * rows * samples,
            transcendentals=0,
        ),
    )(
        block_inverse[0, 0],
        coupling[0, 0],
        data_rhs[0, 0],
        station_seen[0],
        shared_inverse[0],
        walk_weight[None, :],
        shared_rhs[0],
    )
    return coords[None, None], shared.T[None]


def solution(mesh):
    in_specs = (
        P("tech", "chain", "blk", None),
        P("tech", "chain", "blk", None),
        P("tech", "chain", "blk", None),
        P("tech", "chain", "blk"),
        P("chain", None, None),
        P(),
        P("chain", None, None),
    )
    out_specs = (P("tech", "chain", "blk", None), P("chain", None, None))
    return jax.shard_map(
        functools.partial(shards, dict(mesh.shape)),
        mesh=mesh,
        in_specs=in_specs,
        out_specs=out_specs,
        check_vma=False,
    )
```

```python
import functools

import jax
import jax.numpy as jnp
from jax import lax
from jax.experimental import pallas as pl
from jax.experimental.pallas import tpu as pltpu
from jax.sharding import PartitionSpec as P

SWEEPS = 2
HALVES = 1
F32 = jnp.float32
BF16 = jnp.bfloat16
NT = (((1,), (1,)), ((), ()))
TN = (((0,), (0,)), ((), ()))


def split_two(value):
    high = value.astype(BF16)
    return high, (value - high.astype(F32)).astype(BF16)


def kernel(
    weeks,
    groups,
    parts,
    halves,
    chunk,
    tile,
    inverse_hbm,
    coupling_hbm,
    rhs_hbm,
    seen_ref,
    week_inverse_hbm,
    walk_ref,
    week_rhs_hbm,
    coords_hbm,
    shared_ref,
    inverse,
    coupling,
    rhs,
    residual,
    arrived,
    coupling_in,
    coords,
    coords_low,
    seen,
    week_inverse_in,
    week_rhs_in,
    week_rhs,
    inverse_high,
    inverse_low,
    terms,
    terms_low,
    terms_in,
    shared_low,
    current,
    previous,
    later,
    local_sem,
    gather_send,
    gather_recv,
    terms_send,
    terms_recv,
    shared_send,
    shared_recv,
    chain_send,
    chain_recv,
    early_send,
    early_recv,
):
    week = lax.axis_index("chain")
    group = lax.axis_index("tech")
    part = lax.axis_index("blk")
    team = groups * parts
    rank = group * parts + part
    rows = rhs.shape[0]
    piece = current.shape[2]
    half_samples = piece * team
    chunks = rows // chunk
    not_first = week > 0
    not_last = week < weeks - 1

    def member(number):
        return {"tech": number // parts, "blk": lax.rem(number, parts)}

    def ahead(distance):
        return lax.rem(rank + distance, team)

    def behind(distance):
        return lax.rem(rank + team - distance, team)

    def own_slice(half, number):
        return pl.ds(pl.multiple_of(half * half_samples + number * piece, piece), piece)

    def half_slice(half):
        return slice(half * half_samples, (half + 1) * half_samples)

    loads = []
    loads.append(pltpu.make_async_copy(rhs_hbm, rhs, local_sem.at[0]))
    for slot in range(parts):
        column = pl.multiple_of(lax.rem(part + parts - slot, parts) * rows, 128)
        loads.append(
            pltpu.make_async_copy(
                inverse_hbm.at[:, pl.ds(column, rows)], inverse.at[slot], local_sem.at[1 + slot]
            )
        )
    loads.append(pltpu.make_async_copy(coupling_hbm, coupling, local_sem.at[1 + parts]))
    loads.append(
        pltpu.make_async_copy(week_inverse_hbm, week_inverse_in, local_sem.at[2 + parts])
    )
    loads.append(pltpu.make_async_copy(week_rhs_hbm, week_rhs_in, local_sem.at[3 + parts]))
    for load in loads:
        load.start()

    barrier = pltpu.get_barrier_semaphore()
    for distance in range(1, team):
        pl.semaphore_signal(barrier, inc=1, device_id=member(ahead(distance)))

    @pl.when(not_first)
    def _():
        pl.semaphore_signal(barrier, inc=1, device_id={"chain": week - 1})

    @pl.when(not_last)
    def _():
        pl.semaphore_signal(barrier, inc=1, device_id={"chain": week + 1})

    pl.semaphore_wait(
        barrier, team - 1 + not_first.astype(jnp.int32) + not_last.astype(jnp.int32)
    )

    def gather_copy(sweep, half, distance, index):
        span = pl.ds(index * chunk, chunk)
        if sweep == 0:
            source = rhs_hbm.at[span, pl.ds(half * half_samples, half_samples)]
        else:
            source = residual.at[half, span]
        return pltpu.make_async_remote_copy(
            src_ref=source,
            dst_ref=arrived.at[sweep, half, distance - 1, span],
            send_sem=gather_send.at[sweep, half, distance - 1, index],
            recv_sem=gather_recv.at[sweep, half, distance - 1, index],
            device_id={"blk": lax.rem(part + distance, parts)},
        )

    last = pl.ds((chunks - 1) * chunk, chunk)

    def early_copy(distance):
        return pltpu.make_async_remote_copy(
            src_ref=coupling.at[last],
            dst_ref=coupling_in.at[distance - 1],
            send_sem=early_send.at[distance - 1],
            recv_sem=early_recv.at[distance - 1],
            device_id={"blk": lax.rem(part + distance, parts)},
        )

    def terms_copy(sweep, half, distance):
        return pltpu.make_async_remote_copy(
            src_ref=terms_low.at[sweep, own_slice(half, ahead(distance))],
            dst_ref=terms_in.at[sweep, half, distance - 1],
            send_sem=terms_send.at[sweep, half, distance - 1],
            recv_sem=terms_recv.at[sweep, half, distance - 1],
            device_id=member(ahead(distance)),
        )

    def shared_copy(sweep, half, distance, owner):
        return pltpu.make_async_remote_copy(
            src_ref=shared_low.at[sweep, own_slice(half, owner)],
            dst_ref=shared_low.at[sweep, own_slice(half, owner)],
            send_sem=shared_send.at[sweep, half, distance - 1],
            recv_sem=shared_recv.at[sweep, half, distance - 1],
            device_id=member(ahead(distance)),
        )

    def onward_copy(sweep, half):
        return pltpu.make_async_remote_copy(
            src_ref=current.at[sweep, half],
            dst_ref=previous.at[sweep, half],
            send_sem=chain_send.at[sweep, half],
            recv_sem=chain_recv.at[sweep, half],
            device_id={"chain": lax.rem(week + 1, weeks)},
        )

    def backward_copy(sweep, half):
        return pltpu.make_async_remote_copy(
            src_ref=current.at[sweep, half],
            dst_ref=later.at[sweep, half],
            send_sem=chain_send.at[SWEEPS + sweep, half],
            recv_sem=chain_recv.at[SWEEPS + sweep, half],
            device_id={"chain": lax.rem(week + weeks - 1, weeks)},
        )

    def gather_start(sweep, half, index):
        for distance in range(1, parts):
            gather_copy(sweep, half, distance, index).start()

    for half in range(halves):
        for index in range(chunks):
            gather_start(0, half, index)

    stations = seen_ref.shape[1]
    per_station = rows // stations

    @pl.loop(0, rows // tile)
    def _(index):
        start = pl.multiple_of(index * tile, tile)
        row = start + lax.broadcasted_iota(jnp.int32, (tile, stations), 0)
        offset = row - per_station * lax.broadcasted_iota(jnp.int32, (tile, stations), 1)
        inside = jnp.logical_and(offset >= 0, offset < per_station)
        picked = jnp.where(inside, seen_ref[...].astype(F32), 0.0)
        column = jnp.sum(picked, axis=1, keepdims=True)
        seen[pl.ds(start, tile), :] = jnp.broadcast_to(column, (tile, 128))

    for load in loads:
        load.wait()
    week_rhs[...] = jnp.transpose(week_rhs_in[...])
    high, low = split_two(week_inverse_in[...])
    inverse_high[...] = high
    inverse_low[...] = low
    walk = walk_ref[...]

    def solve_shared(value):
        value_high, value_low = split_two(value)
        first = jnp.dot(
            jnp.concatenate([value_high, value_low], axis=0),
            inverse_high[...],
            preferred_element_type=F32,
        )
        second = jnp.dot(value_high, inverse_low[...], preferred_element_type=F32)
        return first[:piece] + (first[piece:] + second)

    def add_columns(half, slot, start, width, block, begin):
        @pl.loop(0, rows // tile)
        def _(index):
            span = pl.ds(pl.multiple_of(index * tile, tile), tile)
            product = jnp.dot(
                inverse[slot, span, start : start + width], block, preferred_element_type=F32
            )
            if begin:
                coords[span, half_slice(half)] = product
            else:
                coords[span, half_slice(half)] += product

    def make_residual(sweep, half):
        for distance in range(1, team):
            shared_copy(sweep - 1, half, distance, behind(distance)).wait_recv()
        for index in range(chunks):
            span = slice(index * chunk, (index + 1) * chunk)
            product = lax.dot_general(
                coupling[span, :],
                shared_low[sweep - 1, half_slice(half), :],
                NT,
                preferred_element_type=F32,
            )
            residual[half, span, :] = (
                rhs[span, half_slice(half)].astype(F32) - product
            ).astype(BF16)
            if index < chunks - 1:
                gather_start(sweep, half, index)

    def make_terms(sweep, half):
        own = rhs[:, half_slice(half)] if sweep == 0 else residual[half]
        add_columns(half, 0, 0, rows, own, True)
        if sweep > 0:
            for distance in range(1, parts):
                if sweep == 1 and half == 0:
                    early_copy(distance).wait_recv()
                product = lax.dot_general(
                    coupling_in[distance - 1],
                    shared_low[sweep - 1, half_slice(half), :],
                    NT,
                    preferred_element_type=F32,
                )
                first = arrived[0, half, distance - 1, last, :].astype(F32)
                block = (first - product).astype(BF16)
                add_columns(half, distance, (chunks - 1) * chunk, chunk, block, False)
        for index in range(chunks if sweep == 0 else chunks - 1):
            span = slice(index * chunk, (index + 1) * chunk)
            for distance in range(1, parts):
                gather_copy(sweep, half, distance, index).wait_recv()
                block = arrived[sweep, half, distance - 1, span, :]
                if sweep == 0 and half == halves - 1 and index == chunks - 1:
                    early_copy(distance).start()
                add_columns(half, distance, index * chunk, chunk, block, False)

        @pl.loop(0, rows // tile)
        def _(index):
            span = pl.ds(pl.multiple_of(index * tile, tile), tile)
            value = coords[span, half_slice(half)] * seen[span, 0:1]
            coords_low[span, :] = value.astype(BF16)
            if sweep == SWEEPS - 1:
                coords[span, half_slice(half)] = value

        product = lax.dot_general(
            coords_low[...], coupling[...], TN, preferred_element_type=F32
        )
        terms[half_slice(half), :] = product
        terms_low[sweep, half_slice(half), :] = product.astype(BF16)
        for distance in range(1, team):
            terms_copy(sweep, half, distance).start()

    def make_shared(sweep, half):
        own = own_slice(half, rank)
        right = week_rhs[own, :] - terms[own, :]
        if sweep > 0:
            @pl.when(not_last)
            def _():
                backward_copy(sweep - 1, half).wait_recv()

            @pl.when(jnp.logical_not(not_last))
            def _():
                later[sweep - 1, half] = jnp.zeros(later.shape[2:], F32)

            right += walk * later[sweep - 1, half]
        for distance in range(1, team):
            terms_copy(sweep, half, distance).wait_recv()
            right -= terms_in[sweep, half, distance - 1].astype(F32)
        current[sweep, half] = solve_shared(right)

        @pl.when(not_first)
        def _():
            onward_copy(sweep, half).wait_recv()
            current[sweep, half] += solve_shared(walk * previous[sweep, half])

        @pl.when(not_last)
        def _():
            onward_copy(sweep, half).start()

        shared_low[sweep, own, :] = current[sweep, half].astype(BF16)
        for distance in range(1, team):
            shared_copy(sweep, half, distance, rank).start()
        if sweep < SWEEPS - 1:
            @pl.when(not_first)
            def _():
                backward_copy(sweep, half).start()

    coords_out = pltpu.make_async_copy(coords, coords_hbm, local_sem.at[0])

    for sweep in range(SWEEPS):
        for half in range(halves):
            make_terms(sweep, half)
            if sweep == SWEEPS - 1 and half == halves - 1:
                coords_out.start()
            if sweep < SWEEPS - 1 and half > 0:
                make_residual(sweep + 1, half - 1)
            make_shared(sweep, half)
        if sweep < SWEEPS - 1:
            make_residual(sweep + 1, halves - 1)
        else:
            for half in range(halves):
                for distance in range(1, team):
                    shared_copy(sweep, half, distance, behind(distance)).wait_recv()

    shared_ref[...] = shared_low[SWEEPS - 1].astype(F32)

    for sweep in range(SWEEPS):
        for half in range(halves):
            for distance in range(1, parts):
                for index in range(chunks if sweep == 0 else chunks - 1):
                    gather_copy(sweep, half, distance, index).wait_send()
            for distance in range(1, team):
                terms_copy(sweep, half, distance).wait_send()
                shared_copy(sweep, half, distance, rank).wait_send()

            @pl.when(not_last)
            def _():
                onward_copy(sweep, half).wait_send()

            if sweep < SWEEPS - 1:
                @pl.when(not_first)
                def _():
                    backward_copy(sweep, half).wait_send()

    for distance in range(1, parts):
        early_copy(distance).wait_send()
    coords_out.wait()


def whole_step(size, limit):
    step = min(size, limit)
    while size % step:
        step -= 16
    return step


def shards(
    mesh_shape,
    block_inverse,
    coupling,
    data_rhs,
    station_seen,
    shared_inverse,
    walk_weight,
    shared_rhs,
):
    weeks, groups, parts = (mesh_shape[axis] for axis in ("chain", "tech", "blk"))
    team = groups * parts
    rows, samples = data_rhs.shape[2:]
    width = shared_inverse.shape[1]
    halves = HALVES
    half_samples = samples // halves
    piece = half_samples // team
    chunk = whole_step(rows, 512)
    tile = whole_step(rows, 512)
    chunks = rows // chunk
    vmem = pl.BlockSpec(memory_space=pltpu.VMEM)
    anywhere = pl.BlockSpec(memory_space=pl.ANY)
    dma = pltpu.SemaphoreType.DMA
    others = max(parts - 1, 1)
    coords, shared = pl.pallas_call(
        functools.partial(kernel, weeks, groups, parts, halves, chunk, tile),
        out_shape=(
            jax.ShapeDtypeStruct((rows, samples), F32),
            jax.ShapeDtypeStruct((samples, width), F32),
        ),
        in_specs=[anywhere] * 3 + [vmem, anywhere, vmem, anywhere],
        out_specs=(anywhere, vmem),
        scratch_shapes=[
            pltpu.VMEM((parts, rows, rows), BF16),
            pltpu.VMEM((rows, width), BF16),
            pltpu.VMEM((rows, samples), BF16),
            pltpu.VMEM((halves, rows, half_samples), BF16),
            pltpu.VMEM((SWEEPS, halves, others, rows, half_samples), BF16),
            pltpu.VMEM((others, chunk, width), BF16),
            pltpu.VMEM((rows, samples), F32),
            pltpu.VMEM((rows, half_samples), BF16),
            pltpu.VMEM((rows, 128), F32),
            pltpu.VMEM((width, width), F32),
            pltpu.VMEM((width, samples), F32),
            pltpu.VMEM((samples, width), F32),
            pltpu.VMEM((width, width), BF16),
            pltpu.VMEM((width, width), BF16),
            pltpu.VMEM((samples, width), F32),
            pltpu.VMEM((SWEEPS, samples, width), BF16),
            pltpu.VMEM((SWEEPS, halves, team - 1, piece, width), BF16),
            pltpu.VMEM((SWEEPS, samples, width), BF16),
            pltpu.VMEM((SWEEPS, halves, piece, width), F32),
            pltpu.VMEM((SWEEPS, halves, piece, width), F32),
            pltpu.VMEM((SWEEPS, halves, piece, width), F32),
            dma((4 + parts,)),
            dma((SWEEPS, halves, others, chunks)),
            dma((SWEEPS, halves, others, chunks)),
            dma((SWEEPS, halves, team - 1)),
            dma((SWEEPS, halves, team - 1)),
            dma((SWEEPS, halves, team - 1)),
            dma((SWEEPS, halves, team - 1)),
            dma((2 * SWEEPS, halves)),
            dma((2 * SWEEPS, halves)),
            dma((others,)),
            dma((others,)),
        ],
        compiler_params=pltpu.CompilerParams(
            collective_id=0, has_side_effects=True, vmem_limit_bytes=60 * 2**20
        ),
        cost_estimate=pl.CostEstimate(
            flops=2 * SWEEPS * rows * samples * (rows * parts + 2 * width),
            bytes_accessed=2 * rows * (rows * parts + width + samples) + 4 * rows * samples,
            transcendentals=0,
        ),
    )(
        block_inverse[0, 0],
        coupling[0, 0],
        data_rhs[0, 0],
        station_seen[0],
        shared_inverse[0],
        walk_weight[None, :],
        shared_rhs[0],
    )
    return coords[None, None], shared.T[None]


def solution(mesh):
    in_specs = (
        P("tech", "chain", "blk", None),
        P("tech", "chain", "blk", None),
        P("tech", "chain", "blk", None),
        P("tech", "chain", "blk"),
        P("chain", None, None),
        P(),
        P("chain", None, None),
    )
    out_specs = (P("tech", "chain", "blk", None), P("chain", None, None))
    return jax.shard_map(
        functools.partial(shards, dict(mesh.shape)),
        mesh=mesh,
        in_specs=in_specs,
        out_specs=out_specs,
        check_vma=False,
    )
```
